32 devices in a mesh: groups: 2 (over x), det: 16 (over z, y, core).
Axes of the slice: x: 2, y: 2, z: 4, core: 2. Of those that a mesh axis runs over, the one named last changes fastest.
Arguments:
- timestream: float32 [2048, 4096], P(('groups', 'det')), parts along dimension 0, may hold values from -31 to 31
- seg_gains: float32 [2048, 4], P(('groups', 'det')), parts along dimension 0, may hold values from 0.25 to 1.75
- seg_bounds: int32 [2048, 3], P(('groups', 'det')), parts along dimension 0, may hold values from 512 to 3584, as said below
- det_band: int32 [2048], P(('groups', 'det')), parts along dimension 0, may hold values from 0 to 1
- band_taps: float32 [2, 32], replicated, may hold values from -1 to 1
- det_wafer: int32 [2048], P(('groups', 'det')), parts along dimension 0, may hold values from 0 to 7, as said below
- wafer_modes: float32 [16, 4096], P('groups'), parts along dimension 0, may hold values from -4 to 4
Outputs:
- covariance: float32 [2048, 1024], P(('groups', 'det')), parts along dimension 0
The draws below stay inside these ranges and needn't reach their ends.
There are 2 independent parts, one for each index of `groups`. The reference program is written for one: setup_inputs(seed, part) draws one part's arguments, and reference() takes and returns one part's arrays. A program takes and returns all parts, laid end to end along the dimension named above; an argument that names none is the same for every part. Nothing has to cross between parts.
Inputs may be any that keep to these rules, and one draw needn't show every extreme that they name: `seg_bounds`: each detector's boundaries rise strictly. `det_wafer`: every wafer has detectors.
All inputs are finite; a program needn't handle non-finite values.
Results may differ from the reference program's by a relative error of at most 0.00086.
Values may be sent and summed in bfloat16 or wider, within the bound.
A program may use at most 128 MiB of HBM per device.

```python
import jax
import jax.numpy as jnp
from jax import lax

NDET = 1024
SAMPLES = 4096
TAPS = 32
NBAND = 2
NSEG = 4
NWAFER = 8


def wafer_and_modes(key):
    chooser = jax.random.randint(jax.random.fold_in(key, 11), (NDET,), 0, 4)
    elsewhere = jax.random.randint(jax.random.fold_in(key, 12), (NDET,), 0, NWAFER)
    home_wafer = jnp.arange(NDET, dtype=jnp.int32) * NWAFER // NDET
    wafer_ids = jnp.where(chooser == 0, elsewhere, home_wafer).astype(jnp.int32)
    mode_draw = jax.random.truncated_normal(jax.random.fold_in(key, 13), -4.0, 4.0, (NWAFER, SAMPLES), jnp.float32)
    return (wafer_ids, mode_draw)


def draw_det_wafer(key, part):
    wafer_ids, mode_draw = wafer_and_modes(key)
    return wafer_ids


def draw_wafer_modes(key, part):
    wafer_ids, mode_draw = wafer_and_modes(key)
    return mode_draw


def draw_timestream(key, part):
    wafer_ids, mode_draw = wafer_and_modes(key)
    key = jax.random.fold_in(key, 5)
    level_rows = 1.0 + 2.0 * jnp.arange(NDET, dtype=jnp.float32) / (NDET - 1)
    noise_part = jax.random.truncated_normal(jax.random.fold_in(key, 1), -4.0, 4.0, (NDET, SAMPLES), jnp.float32)
    strength = 1.5
    return level_rows[:, None] * noise_part + strength * mode_draw[wafer_ids]


def draw_seg_bounds(key, part):
    key = jax.random.fold_in(key, 7)
    lengths = jax.random.randint(key, (NDET, 3), SAMPLES // 8, SAMPLES // 4 + 1)
    first = lengths[:, 0]
    second = lengths[:, 0] + lengths[:, 1]
    third = SAMPLES - lengths[:, 2]
    return jnp.stack([first, second, third], axis=1).astype(jnp.int32)


def touch_ends(values, own_key, low, high):
    longest = values.shape.index(max(values.shape))
    spots = []
    for shift in (0, 1):
        where = [jax.random.randint(jax.random.fold_in(own_key, axis), (), 0, length) for axis, length in enumerate(values.shape)]
        where[longest] = (where[longest] + shift) % values.shape[longest]
        spots.append(tuple(where))
    return values.at[spots[0]].set(low).at[spots[1]].set(high)


def bell_draw(rng, shape, spread, limit, kind=jnp.bfloat16):
    entries = spread * jax.random.normal(rng, shape, jnp.float32)
    return jnp.clip(entries, min=-limit, max=limit).astype(kind)


def setup_inputs(seed: int = 0, part: int = 0) -> dict:
    keys = jax.random.split(jax.random.key(seed), 8)
    part_keys = jax.random.split(jax.random.fold_in(keys[7], part), 8)
    timestream = draw_timestream(jax.random.fold_in(jax.random.fold_in(keys[7], part), 71), part)
    seg_gains = jnp.clip(1.0 + 0.15 * jax.random.normal(part_keys[1], (NDET, NSEG), jnp.float32), 0.25, 1.75)
    seg_bounds = draw_seg_bounds(jax.random.fold_in(jax.random.fold_in(keys[7], part), 71), part)
    det_band = touch_ends(jax.random.randint(part_keys[3], (NDET,), 0, NBAND), jax.random.fold_in(part_keys[3], 1), 0, NBAND - 1).astype(jnp.int32)
    band_taps = bell_draw(keys[4], (NBAND, TAPS), TAPS ** -0.5, 1.0, jnp.float32)
    det_wafer = draw_det_wafer(jax.random.fold_in(jax.random.fold_in(keys[7], part), 71), part)
    wafer_modes = draw_wafer_modes(jax.random.fold_in(jax.random.fold_in(keys[7], part), 71), part)
    return dict(timestream=timestream, seg_gains=seg_gains, seg_bounds=seg_bounds, det_band=det_band, band_taps=band_taps, det_wafer=det_wafer, wafer_modes=wafer_modes)


def filter_rows(timestream, seg_gains, seg_bounds, det_band, band_taps):
    det_rows = timestream.shape[0]
    samples = timestream.shape[1]
    tap_count = band_taps.shape[1]
    moments = jnp.arange(samples, dtype=jnp.int32)
    segment = jnp.zeros((det_rows, samples), jnp.int32)
    for column in range(seg_bounds.shape[1]):
        segment = segment + (moments[None, :] >= seg_bounds[:, column:column + 1]).astype(jnp.int32)
    profile = jnp.zeros((det_rows, samples), jnp.float32)
    for column in range(seg_gains.shape[1]):
        profile = profile + jnp.where(segment == column, seg_gains[:, column:column + 1], 0.0)
    scaled = timestream * profile
    own_taps = jnp.zeros((det_rows, tap_count), jnp.float32)
    for band_index in range(band_taps.shape[0]):
        own_taps = own_taps + jnp.where(det_band[:, None] == band_index, band_taps[band_index][None, :], 0.0)
    padded = jnp.pad(scaled, ((0, 0), (tap_count - 1, 0)))
    kernel = own_taps[:, ::-1][:, None, :]
    result = lax.conv_general_dilated(padded[None], kernel, (1,), "VALID", dimension_numbers=("NCH", "OIH", "NCH"), feature_group_count=det_rows, precision=lax.Precision.HIGHEST)
    return result[0]


def project(filtered, det_wafer, wafer_modes):
    onehot = (det_wafer[:, None] == jnp.arange(wafer_modes.shape[0], dtype=jnp.int32)[None, :]).astype(jnp.float32)
    own_mode = jnp.dot(onehot, wafer_modes, precision=lax.Precision.HIGHEST)
    coupling = jnp.mean(filtered * own_mode, axis=1, keepdims=True) / (jnp.mean(own_mode * own_mode, axis=1, keepdims=True) + 1e-6)
    return (filtered - coupling * own_mode).astype(jnp.bfloat16)


def reference(timestream, seg_gains, seg_bounds, det_band, band_taps, det_wafer, wafer_modes):
    cleaned = project(filter_rows(timestream, seg_gains, seg_bounds, det_band, band_taps), det_wafer, wafer_modes)
    widened = cleaned.astype(jnp.float32)
    mean_power = jnp.sum(widened * widened) / (NDET * SAMPLES)
    covar = jnp.dot(cleaned, cleaned.T, preferred_element_type=jnp.float32)
    return covar / (SAMPLES * mean_power)
```

```python
import functools

import jax
import jax.numpy as jnp
from jax import lax
from jax.experimental import pallas as pl
from jax.experimental.pallas import tpu as pltpu
from jax.sharding import PartitionSpec as P

F32 = jnp.float32
BF16 = jnp.bfloat16
LANES = 128
MESH = pl.DeviceIdType.MESH


def split2(x):
    high = x.astype(BF16)
    return high, (x - high.astype(F32)).astype(BF16)


def mm(a, b):
    return jnp.dot(a, b, preferred_element_type=F32)


def mm_t(a, b):
    return lax.dot_general(a, b, (((1,), (1,)), ((), ())), preferred_element_type=F32)


def kernel(
    n, folded, groups_of_rows,
    ts_ref, gains_ref, bounds_ref, band_ref, taps_ref, wafer_ref, modes_ref,
    out_ref,
    own_ref, xh_ref, xm_ref, y_ref,
    a_ref, b_ref, p_ref, t_ref, sib_ref, got_ref, ssq_ref,
    sib_send, sib_recv, ring_send, ring_recv,
    psend, precv, tsend, trecv, qsend, qrecv,
):
    rows, samples = ts_ref.shape
    half = samples // 2
    chips = n // 2
    hops = chips // 2
    blocks = samples // LANES
    part = rows // groups_of_rows
    bands, taps = taps_ref.shape
    wafers = modes_ref.shape[0]

    me = lax.axis_index("det")
    core = lax.rem(me, 2)
    chip = me // 2
    if folded:
        odd = lax.rem(chip, 2)
        ring = (1 - odd) * (chip // 2) + odd * (chips - 1 - chip // 2)
    else:
        ring = chip

    def chip_at(pos):
        pos = lax.rem(pos + 2 * chips, chips)
        if not folded:
            return pos
        late = pos // (chips // 2)
        return (1 - late) * 2 * pos + late * (2 * (chips - 1 - pos) + 1)

    step = 1 - 2 * core

    barrier = pltpu.get_barrier_semaphore()

    def greet(i, carry):
        pl.semaphore_signal(
            barrier, inc=1, device_id={"det": lax.rem(me + i, n)}, device_id_type=MESH
        )
        return carry

    lax.fori_loop(1, n, greet, 0)

    depth = LANES + taps
    lag = (
        lax.broadcasted_iota(jnp.int32, (depth, LANES), 1)
        + taps
        - lax.broadcasted_iota(jnp.int32, (depth, LANES), 0)
    )
    mats = []
    for band in range(bands):
        mat = jnp.zeros((depth, LANES), F32)
        for k in range(taps):
            mat = jnp.where(lag == k, taps_ref[band, k], mat)
        mats.append(jnp.concatenate([jnp.zeros((LANES - taps, LANES), F32), mat], axis=0))
    toep_h, toep_m = split2(jnp.concatenate(mats, axis=1))

    eye = lax.broadcasted_iota(jnp.int32, (rows, rows), 0) == lax.broadcasted_iota(
        jnp.int32, (rows, rows), 1
    )

    def column(ref):
        return jnp.sum(jnp.where(eye, ref[...].astype(F32), 0.0), axis=1, keepdims=True)

    band_col = column(band_ref)
    wafer_col = column(wafer_ref)

    modes = modes_ref[...]
    m1 = modes.astype(BF16).astype(F32)
    m2 = (modes - m1).astype(BF16).astype(F32)
    m3 = modes - m1 - m2
    stack = jnp.concatenate([m1, m2, m3], axis=0).astype(BF16)
    which = lax.rem(lax.broadcasted_iota(jnp.int32, (rows, 3 * wafers), 1), wafers)
    onehot = jnp.where(which.astype(F32) == wafer_col, 1.0, 0.0).astype(BF16)
    own_ref[...] = mm(onehot, stack)

    def ring_copy(d, g, who):
        span = pl.ds(g * part, part)
        src = a_ref.at[who, span] if d == 0 else b_ref.at[d - 1, who, span]
        return pltpu.make_async_remote_copy(
            src_ref=src,
            dst_ref=b_ref.at[d, who, span],
            send_sem=ring_send.at[d, who, g],
            recv_sem=ring_recv.at[d, who, g],
            device_id={"det": 2 * chip_at(ring + step) + core},
            device_id_type=MESH,
        )

    def sib_copy(g):
        span = pl.ds(g * part, part)
        return pltpu.make_async_remote_copy(
            src_ref=a_ref.at[2, span],
            dst_ref=a_ref.at[core, span],
            send_sem=sib_send.at[g],
            recv_sem=sib_recv.at[g],
            device_id={"det": 2 * chip + 1 - core},
            device_id_type=MESH,
        )

    def sib_arrival(g):
        span = pl.ds(g * part, part)
        return pltpu.make_async_remote_copy(
            src_ref=a_ref.at[2, span],
            dst_ref=a_ref.at[1 - core, span],
            send_sem=sib_send.at[g],
            recv_sem=sib_recv.at[g],
            device_id={"det": 2 * chip + 1 - core},
            device_id_type=MESH,
        )

    power = jnp.zeros((8, LANES), F32)
    sends = []
    for g in range(groups_of_rows):
        lo, hi = g * part, (g + 1) * part
        bound = [bounds_ref[lo:hi, c : c + 1] for c in range(bounds_ref.shape[1])]
        gain = [gains_ref[lo:hi, c : c + 1] for c in range(gains_ref.shape[1])]
        in_band = [band_col[lo:hi] == float(band) for band in range(bands)]
        xh_ref[0:part, 0:LANES] = jnp.zeros((part, LANES), BF16)
        xm_ref[0:part, 0:LANES] = jnp.zeros((part, LANES), BF16)
        for blk in range(blocks):
            when = lax.broadcasted_iota(jnp.int32, (part, LANES), 1) + blk * LANES
            prof = jnp.broadcast_to(gain[0], (part, LANES))
            for c, edge in enumerate(bound):
                prof = jnp.where(when >= edge, gain[c + 1], prof)
            xh, xm = split2(ts_ref[lo:hi, blk * LANES : (blk + 1) * LANES] * prof)
            at = blk * part
            xh_ref[at : at + part, LANES:] = xh
            xm_ref[at : at + part, LANES:] = xm
            if blk + 1 < blocks:
                xh_ref[at + part : at + 2 * part, 0:LANES] = xh
                xm_ref[at + part : at + 2 * part, 0:LANES] = xm
        y_ref[...] = mm(xh_ref[...], toep_h) + (
            mm(xh_ref[...], toep_m) + mm(xm_ref[...], toep_h)
        )
        cross = jnp.zeros((part, LANES), F32)
        norm = jnp.zeros((part, LANES), F32)
        for blk in range(blocks):
            at = blk * part
            filt = y_ref[at : at + part, 0:LANES]
            for band in range(1, bands):
                filt = jnp.where(
                    in_band[band], y_ref[at : at + part, band * LANES : (band + 1) * LANES], filt
                )
            y_ref[at : at + part, 0:LANES] = filt
            mode = own_ref[lo:hi, blk * LANES : (blk + 1) * LANES]
            cross = cross + filt * mode
            norm = norm + mode * mode
        coupling = (jnp.sum(cross, axis=1, keepdims=True) / samples) / (
            jnp.sum(norm, axis=1, keepdims=True) / samples + 1e-06
        )
        sq = jnp.zeros((part, LANES), F32)
        for blk in range(blocks):
            at = blk * part
            second = blk >= blocks // 2
            slot = (2 - core) if second else 2 * core
            mode = own_ref[lo:hi, blk * LANES : (blk + 1) * LANES]
            clean = (y_ref[at : at + part, 0:LANES] - coupling * mode).astype(BF16)
            col = blk * LANES - (half if second else 0)
            a_ref[slot, lo:hi, col : col + LANES] = clean
            wide = clean.astype(F32)
            sq = sq + wide * wide
        for i in range(part // 8):
            power = power + sq[8 * i : 8 * i + 8]
        if g == 0:
            pl.semaphore_wait(barrier, n - 1)
        sib = sib_copy(g)
        sib.start()
        first = ring_copy(0, g, core)
        first.start()
        sends += [sib, first]

    for g in range(groups_of_rows):
        sib_arrival(g).wait_recv()
        second = ring_copy(0, g, 1 - core)
        second.start()
        sends.append(second)

    ssq_ref[0] = power

    def power_copy(i):
        return pltpu.make_async_remote_copy(
            src_ref=ssq_ref.at[0],
            dst_ref=ssq_ref.at[i],
            send_sem=qsend.at[i],
            recv_sem=qrecv.at[i],
            device_id={"det": lax.rem(me + i, n)},
            device_id_type=MESH,
        )

    def power_start(i, carry):
        power_copy(i).start()
        return carry

    def power_wait(i, carry):
        power_copy(i).wait()
        return carry

    lax.fori_loop(1, n, power_start, 0)

    def give_sibling(d):
        return pltpu.make_async_remote_copy(
            src_ref=p_ref.at[d, 1 - core],
            dst_ref=sib_ref.at[d],
            send_sem=psend.at[d],
            recv_sem=precv.at[d],
            device_id={"det": 2 * chip + 1 - core},
            device_id_type=MESH,
        )

    def give_turned(d, to):
        return pltpu.make_async_remote_copy(
            src_ref=t_ref.at[d - 1, to],
            dst_ref=got_ref.at[core, d - 1],
            send_sem=tsend.at[d - 1, to],
            recv_sem=trecv.at[core, d - 1],
            device_id={"det": 2 * chip_at(ring - step * d) + to},
            device_id_type=MESH,
        )

    def take_turned(who, d):
        return pltpu.make_async_remote_copy(
            src_ref=t_ref.at[d - 1, 0],
            dst_ref=got_ref.at[who, d - 1],
            send_sem=tsend.at[d - 1, 0],
            recv_sem=trecv.at[who, d - 1],
            device_id={"det": 2 * chip + 1 - core},
            device_id_type=MESH,
        )

    mine = a_ref[0:2].reshape(2 * rows, half)

    def product(d):
        block = mine if d == 0 else b_ref[d - 1].reshape(2 * rows, half)
        prod = mm_t(mine, block)
        p_ref[d, 0] = prod[0:rows]
        p_ref[d, 1] = prod[rows:]
        give = give_sibling(d)
        give.start()
        sends.append(give)
        if 0 < d < hops:
            turned = prod.T
            t_ref[d - 1, 0] = turned[0:rows]
            t_ref[d - 1, 1] = turned[rows:]
            for to in range(2):
                give = give_turned(d, to)
                give.start()
                sends.append(give)

    product(0)
    for d in range(1, hops + 1):
        for flip in range(2):
            who = core if flip == 0 else 1 - core
            for g in range(groups_of_rows):
                ring_copy(d - 1, g, who).wait_recv()
                if d < hops:
                    onward = ring_copy(d, g, who)
                    onward.start()
                    sends.append(onward)
        product(d)

    lax.fori_loop(1, n, power_wait, 0)

    def add_power(i, total):
        return total + ssq_ref[i]

    total = jnp.sum(lax.fori_loop(1, n, add_power, power))
    mean_power = total / float(rows * n * samples)
    scale = 1.0 / (samples * jnp.full((rows, LANES), mean_power, F32))

    def put(pos, value):
        col = pl.multiple_of(chip_at(pos) * (2 * rows), 2 * rows)
        out_ref[:, pl.ds(col, 2 * rows)] = value * scale

    for d in range(hops + 1):
        give_sibling(d).wait_recv()
        if d == 0 or d == hops:
            put(ring + d, p_ref[d, core] + sib_ref[d])
        else:
            take_turned(1 - core, d).wait_recv()
            put(ring - step * d, p_ref[d, core] + got_ref[1 - core, d - 1])
            take_turned(core, d).wait_recv()
            put(ring + step * d, sib_ref[d] + got_ref[core, d - 1])

    for copy in sends:
        copy.wait_send()


def on_device(
    n, folded, timestream, seg_gains, seg_bounds, det_band, band_taps, det_wafer, wafer_modes
):
    rows, samples = timestream.shape
    half = samples // 2
    hops = n // 4
    pieces = 2
    part = rows // pieces
    bands = band_taps.shape[0]
    vmem = pl.BlockSpec(memory_space=pltpu.VMEM)
    dma = pltpu.SemaphoreType.DMA
    return pl.pallas_call(
        functools.partial(kernel, n, folded, pieces),
        out_shape=jax.ShapeDtypeStruct((rows, rows * n), F32),
        in_specs=[vmem] * 4 + [pl.BlockSpec(memory_space=pltpu.SMEM)] + [vmem] * 2,
        out_specs=vmem,
        scratch_shapes=[
            pltpu.VMEM((rows, samples), F32),
            pltpu.VMEM((part * samples // LANES, 2 * LANES), BF16),
            pltpu.VMEM((part * samples // LANES, 2 * LANES), BF16),
            pltpu.VMEM((part * samples // LANES, bands * LANES), F32),
            pltpu.VMEM((3, rows, half), BF16),
            pltpu.VMEM((hops, 2, rows, half), BF16),
            pltpu.VMEM((hops + 1, 2, rows, 2 * rows), F32),
            pltpu.VMEM((hops - 1, 2, rows, 2 * rows), F32),
            pltpu.VMEM((hops + 1, rows, 2 * rows), F32),
            pltpu.VMEM((2, hops - 1, rows, 2 * rows), F32),
            pltpu.VMEM((n, 8, LANES), F32),
            dma((pieces,)),
            dma((pieces,)),
            dma((hops, 2, pieces)),
            dma((hops, 2, pieces)),
            dma((hops + 1,)),
            dma((hops + 1,)),
            dma((hops - 1, 2)),
            dma((2, hops - 1)),
            dma((n,)),
            dma((n,)),
        ],
        compiler_params=pltpu.CompilerParams(
            collective_id=0, has_side_effects=True, vmem_limit_bytes=48 * 1024 * 1024
        ),
    )(
        timestream,
        seg_gains,
        seg_bounds,
        det_band.reshape(1, rows),
        band_taps,
        det_wafer.reshape(1, rows),
        wafer_modes,
    )


def solution(mesh):
    n = mesh.shape["det"]
    folded = mesh.shape["groups"] == 2
    return jax.shard_map(
        functools.partial(on_device, n, folded),
        mesh=mesh,
        in_specs=(
            P(("groups", "det"), None),
            P(("groups", "det"), None),
            P(("groups", "det"), None),
            P(("groups", "det")),
            P(),
            P(("groups", "det")),
            P("groups", None),
        ),
        out_specs=P(("groups", "det"), None),
        check_vma=False,
    )
```

```python
import functools

import jax
import jax.numpy as jnp
from jax import lax
from jax.experimental import pallas as pl
from jax.experimental.pallas import tpu as pltpu
from jax.sharding import PartitionSpec as P

F32 = jnp.float32
BF16 = jnp.bfloat16
LANES = 128
MESH = pl.DeviceIdType.MESH


def split2(x):
    high = x.astype(BF16)
    return high, (x - high.astype(F32)).astype(BF16)


def mm(a, b):
    return jnp.dot(a, b, preferred_element_type=F32)


def mm_t(a, b):
    return lax.dot_general(a, b, (((1,), (1,)), ((), ())), preferred_element_type=F32)


def kernel(
    n, folded, groups_of_rows,
    ts_hbm, gains_hbm, bounds_hbm, band_hbm, taps_hbm, wafer_hbm, modes_hbm,
    out_ref,
    ts_ref, gains_ref, bounds_ref, band_ref, taps_ref, wafer_ref, modes_ref, in_sem,
    own_ref, xh_ref, xm_ref, y_ref,
    a_ref, b_ref, p_ref, t_ref, sib_ref, got_ref, ssq_ref,
    sib_send, sib_recv, ring_send, ring_recv,
    psend, precv, tsend, trecv, qsend, qrecv,
):
    rows, samples = ts_hbm.shape
    half = samples // 2
    chips = n // 2
    hops = chips // 2
    blocks = samples // LANES
    part = rows // groups_of_rows
    bands, taps = taps_ref.shape
    wafers = modes_ref.shape[0]

    me = lax.axis_index("det")
    core = lax.rem(me, 2)
    chip = me // 2
    if folded:
        odd = lax.rem(chip, 2)
        ring = (1 - odd) * (chip // 2) + odd * (chips - 1 - chip // 2)
    else:
        ring = chip

    def chip_at(pos):
        pos = lax.rem(pos + 2 * chips, chips)
        if not folded:
            return pos
        late = pos // (chips // 2)
        return (1 - late) * 2 * pos + late * (2 * (chips - 1 - pos) + 1)

    step = 1 - 2 * core

    barrier = pltpu.get_barrier_semaphore()

    def greet(i, carry):
        pl.semaphore_signal(
            barrier, inc=1, device_id={"det": lax.rem(me + i, n)}, device_id_type=MESH
        )
        return carry

    lax.fori_loop(1, n, greet, 0)

    small = [
        pltpu.make_async_copy(src, dst, in_sem.at[i])
        for i, (src, dst) in enumerate(
            (
                (taps_hbm, taps_ref),
                (modes_hbm, modes_ref),
                (band_hbm, band_ref),
                (wafer_hbm, wafer_ref),
                (gains_hbm, gains_ref),
                (bounds_hbm, bounds_ref),
            )
        )
    ]
    large = [
        pltpu.make_async_copy(
            ts_hbm.at[pl.ds(g * part, part)],
            ts_ref.at[pl.ds(g * part, part)],
            in_sem.at[len(small) + g],
        )
        for g in range(groups_of_rows)
    ]
    for copy in small + large:
        copy.start()
    small[0].wait()

    depth = LANES + taps
    lag = (
        lax.broadcasted_iota(jnp.int32, (depth, LANES), 1)
        + taps
        - lax.broadcasted_iota(jnp.int32, (depth, LANES), 0)
    )
    mats = []
    for band in range(bands):
        mat = jnp.zeros((depth, LANES), F32)
        for k in range(taps):
            mat = jnp.where(lag == k, taps_ref[band, k], mat)
        mats.append(jnp.concatenate([jnp.zeros((LANES - taps, LANES), F32), mat], axis=0))
    toep_h, toep_m = split2(jnp.concatenate(mats, axis=1))

    for copy in small[1:]:
        copy.wait()

    eye = lax.broadcasted_iota(jnp.int32, (rows, rows), 0) == lax.broadcasted_iota(
        jnp.int32, (rows, rows), 1
    )

    def column(ref, i=0):
        row = ref[i : i + 1, :].astype(F32)
        return jnp.sum(jnp.where(eye, row, 0.0), axis=1, keepdims=True)

    band_col = column(band_ref)
    wafer_col = column(wafer_ref)
    gain_cols = [column(gains_ref, i) for i in range(gains_ref.shape[0])]
    bound_cols = [column(bounds_ref, i).astype(jnp.int32) for i in range(bounds_ref.shape[0])]

    modes = modes_ref[...]
    m1 = modes.astype(BF16).astype(F32)
    m2 = (modes - m1).astype(BF16).astype(F32)
    m3 = modes - m1 - m2
    stack = jnp.concatenate([m1, m2, m3], axis=0).astype(BF16)
    which = lax.rem(lax.broadcasted_iota(jnp.int32, (rows, 3 * wafers), 1), wafers)
    onehot = jnp.where(which.astype(F32) == wafer_col, 1.0, 0.0).astype(BF16)
    own_ref[...] = mm(onehot, stack)

    def ring_copy(d, g, who):
        span = pl.ds(g * part, part)
        src = a_ref.at[who, span] if d == 0 else b_ref.at[d - 1, who, span]
        return pltpu.make_async_remote_copy(
            src_ref=src,
            dst_ref=b_ref.at[d, who, span],
            send_sem=ring_send.at[d, who, g],
            recv_sem=ring_recv.at[d, who, g],
            device_id={"det": 2 * chip_at(ring + step) + core},
            device_id_type=MESH,
        )

    def sib_copy(g):
        span = pl.ds(g * part, part)
        return pltpu.make_async_remote_copy(
            src_ref=a_ref.at[2, span],
            dst_ref=a_ref.at[core, span],
            send_sem=sib_send.at[g],
            recv_sem=sib_recv.at[g],
            device_id={"det": 2 * chip + 1 - core},
            device_id_type=MESH,
        )

    def sib_arrival(g):
        span = pl.ds(g * part, part)
        return pltpu.make_async_remote_copy(
            src_ref=a_ref.at[2, span],
            dst_ref=a_ref.at[1 - core, span],
            send_sem=sib_send.at[g],
            recv_sem=sib_recv.at[g],
            device_id={"det": 2 * chip + 1 - core},
            device_id_type=MESH,
        )

    power = jnp.zeros((8, LANES), F32)
    sends = []
    for g in range(groups_of_rows):
        lo, hi = g * part, (g + 1) * part
        bound = [col[lo:hi] for col in bound_cols]
        gain = [col[lo:hi] for col in gain_cols]
        in_band = [band_col[lo:hi] == float(band) for band in range(bands)]
        large[g].wait()
        xh_ref[0:part, 0:LANES] = jnp.zeros((part, LANES), BF16)
        xm_ref[0:part, 0:LANES] = jnp.zeros((part, LANES), BF16)
        for blk in range(blocks):
            when = lax.broadcasted_iota(jnp.int32, (part, LANES), 1) + blk * LANES
            prof = jnp.broadcast_to(gain[0], (part, LANES))
            for c, edge in enumerate(bound):
                prof = jnp.where(when >= edge, gain[c + 1], prof)
            xh, xm = split2(ts_ref[lo:hi, blk * LANES : (blk + 1) * LANES] * prof)
            at = blk * part
            xh_ref[at : at + part, LANES:] = xh
            xm_ref[at : at + part, LANES:] = xm
            if blk + 1 < blocks:
                xh_ref[at + part : at + 2 * part, 0:LANES] = xh
                xm_ref[at + part : at + 2 * part, 0:LANES] = xm
        y_ref[...] = mm(xh_ref[...], toep_h) + (
            mm(xh_ref[...], toep_m) + mm(xm_ref[...], toep_h)
        )
        cross = jnp.zeros((part, LANES), F32)
        norm = jnp.zeros((part, LANES), F32)
        for blk in range(blocks):
            at = blk * part
            filt = y_ref[at : at + part, 0:LANES]
            for band in range(1, bands):
                filt = jnp.where(
                    in_band[band], y_ref[at : at + part, band * LANES : (band + 1) * LANES], filt
                )
            y_ref[at : at + part, 0:LANES] = filt
            mode = own_ref[lo:hi, blk * LANES : (blk + 1) * LANES]
            cross = cross + filt * mode
            norm = norm + mode * mode
        coupling = (jnp.sum(cross, axis=1, keepdims=True) / samples) / (
            jnp.sum(norm, axis=1, keepdims=True) / samples + 1e-06
        )
        sq = jnp.zeros((part, LANES), F32)
        for blk in range(blocks):
            at = blk * part
            second = blk >= blocks // 2
            slot = (2 - core) if second else 2 * core
            mode = own_ref[lo:hi, blk * LANES : (blk + 1) * LANES]
            clean = (y_ref[at : at + part, 0:LANES] - coupling * mode).astype(BF16)
            col = blk * LANES - (half if second else 0)
            a_ref[slot, lo:hi, col : col + LANES] = clean
            wide = clean.astype(F32)
            sq = sq + wide * wide
        for i in range(part // 8):
            power = power + sq[8 * i : 8 * i + 8]
        if g == 0:
            pl.semaphore_wait(barrier, n - 1)
        sib = sib_copy(g)
        sib.start()
        first = ring_copy(0, g, core)
        first.start()
        sends += [sib, first]

    for g in range(groups_of_rows):
        sib_arrival(g).wait_recv()
        second = ring_copy(0, g, 1 - core)
        second.start()
        sends.append(second)

    ssq_ref[0] = power

    def power_copy(i):
        return pltpu.make_async_remote_copy(
            src_ref=ssq_ref.at[0],
            dst_ref=ssq_ref.at[i],
            send_sem=qsend.at[i],
            recv_sem=qrecv.at[i],
            device_id={"det": lax.rem(me + i, n)},
            device_id_type=MESH,
        )

    def power_start(i, carry):
        power_copy(i).start()
        return carry

    def power_wait(i, carry):
        power_copy(i).wait()
        return carry

    lax.fori_loop(1, n, power_start, 0)

    def give_sibling(d):
        return pltpu.make_async_remote_copy(
            src_ref=p_ref.at[d, 1 - core],
            dst_ref=sib_ref.at[d],
            send_sem=psend.at[d],
            recv_sem=precv.at[d],
            device_id={"det": 2 * chip + 1 - core},
            device_id_type=MESH,
        )

    def give_turned(d, to):
        return pltpu.make_async_remote_copy(
            src_ref=t_ref.at[d - 1, to],
            dst_ref=got_ref.at[core, d - 1],
            send_sem=tsend.at[d - 1, to],
            recv_sem=trecv.at[core, d - 1],
            device_id={"det": 2 * chip_at(ring - step * d) + to},
            device_id_type=MESH,
        )

    def take_turned(who, d):
        return pltpu.make_async_remote_copy(
            src_ref=t_ref.at[d - 1, 0],
            dst_ref=got_ref.at[who, d - 1],
            send_sem=tsend.at[d - 1, 0],
            recv_sem=trecv.at[who, d - 1],
            device_id={"det": 2 * chip + 1 - core},
            device_id_type=MESH,
        )

    mine = a_ref[0:2].reshape(2 * rows, half)

    def product(d):
        block = mine if d == 0 else b_ref[d - 1].reshape(2 * rows, half)
        prod = mm_t(mine, block)
        p_ref[d, 0] = prod[0:rows]
        p_ref[d, 1] = prod[rows:]
        give = give_sibling(d)
        give.start()
        sends.append(give)
        if 0 < d < hops:
            turned = prod.T
            t_ref[d - 1, 0] = turned[0:rows]
            t_ref[d - 1, 1] = turned[rows:]
            for to in range(2):
                give = give_turned(d, to)
                give.start()
                sends.append(give)

    product(0)
    for d in range(1, hops + 1):
        for flip in range(2):
            who = core if flip == 0 else 1 - core
            for g in range(groups_of_rows):
                ring_copy(d - 1, g, who).wait_recv()
                if d < hops:
                    onward = ring_copy(d, g, who)
                    onward.start()
                    sends.append(onward)
        product(d)

    lax.fori_loop(1, n, power_wait, 0)

    def add_power(i, total):
        return total + ssq_ref[i]

    total = jnp.sum(lax.fori_loop(1, n, add_power, power))
    mean_power = total / float(rows * n * samples)
    scale = 1.0 / (samples * jnp.full((rows, LANES), mean_power, F32))

    def put(pos, value):
        col = pl.multiple_of(chip_at(pos) * (2 * rows), 2 * rows)
        out_ref[:, pl.ds(col, 2 * rows)] = value * scale

    for d in range(hops + 1):
        give_sibling(d).wait_recv()
        if d == 0 or d == hops:
            put(ring + d, p_ref[d, core] + sib_ref[d])
        else:
            take_turned(1 - core, d).wait_recv()
            put(ring - step * d, p_ref[d, core] + got_ref[1 - core, d - 1])
            take_turned(core, d).wait_recv()
            put(ring + step * d, sib_ref[d] + got_ref[core, d - 1])

    for copy in sends:
        copy.wait_send()


def on_device(
    n, folded, timestream, seg_gains, seg_bounds, det_band, band_taps, det_wafer, wafer_modes
):
    rows, samples = timestream.shape
    half = samples // 2
    hops = n // 4
    pieces = 2
    part = rows // pieces
    bands = band_taps.shape[0]
    hbm = pl.BlockSpec(memory_space=pltpu.HBM)
    dma = pltpu.SemaphoreType.DMA
    return pl.pallas_call(
        functools.partial(kernel, n, folded, pieces),
        out_shape=jax.ShapeDtypeStruct((rows, rows * n), F32),
        in_specs=[hbm] * 7,
        out_specs=pl.BlockSpec(memory_space=pltpu.VMEM),
        scratch_shapes=[
            pltpu.VMEM((rows, samples), F32),
            pltpu.VMEM(seg_gains.shape[::-1], F32),
            pltpu.VMEM(seg_bounds.shape[::-1], jnp.int32),
            pltpu.VMEM((1, rows), jnp.int32),
            pltpu.SMEM(band_taps.shape, F32),
            pltpu.VMEM((1, rows), jnp.int32),
            pltpu.VMEM(wafer_modes.shape, F32),
            dma((6 + pieces,)),
            pltpu.VMEM((rows, samples), F32),
            pltpu.VMEM((part * samples // LANES, 2 * LANES), BF16),
            pltpu.VMEM((part * samples // LANES, 2 * LANES), BF16),
            pltpu.VMEM((part * samples // LANES, bands * LANES), F32),
            pltpu.VMEM((3, rows, half), BF16),
            pltpu.VMEM((hops, 2, rows, half), BF16),
            pltpu.VMEM((hops + 1, 2, rows, 2 * rows), F32),
            pltpu.VMEM((hops - 1, 2, rows, 2 * rows), F32),
            pltpu.VMEM((hops + 1, rows, 2 * rows), F32),
            pltpu.VMEM((2, hops - 1, rows, 2 * rows), F32),
            pltpu.VMEM((n, 8, LANES), F32),
            dma((pieces,)),
            dma((pieces,)),
            dma((hops, 2, pieces)),
            dma((hops, 2, pieces)),
            dma((hops + 1,)),
            dma((hops + 1,)),
            dma((hops - 1, 2)),
            dma((2, hops - 1)),
            dma((n,)),
            dma((n,)),
        ],
        compiler_params=pltpu.CompilerParams(
            collective_id=0, has_side_effects=True, vmem_limit_bytes=63 * 1024 * 1024
        ),
    )(
        timestream,
        seg_gains.T,
        seg_bounds.T,
        det_band.reshape(1, rows),
        band_taps,
        det_wafer.reshape(1, rows),
        wafer_modes,
    )


def solution(mesh):
    n = mesh.shape["det"]
    folded = mesh.shape["groups"] == 2
    return jax.shard_map(
        functools.partial(on_device, n, folded),
        mesh=mesh,
        in_specs=(
            P(("groups", "det"), None),
            P(("groups", "det"), None),
            P(("groups", "det"), None),
            P(("groups", "det")),
            P(),
            P(("groups", "det")),
            P("groups", None),
        ),
        out_specs=P(("groups", "det"), None),
        check_vma=False,
    )
```

```python
import functools

import jax
import jax.numpy as jnp
from jax import lax
from jax.experimental import pallas as pl
from jax.experimental.pallas import tpu as pltpu
from jax.sharding import PartitionSpec as P

F32 = jnp.float32
BF16 = jnp.bfloat16
LANES = 128
MESH = pl.DeviceIdType.MESH


def split2(x):
    high = x.astype(BF16)
    return high, (x - high.astype(F32)).astype(BF16)


def mm(a, b):
    return jnp.dot(a, b, preferred_element_type=F32)


def mm_t(a, b):
    return lax.dot_general(a, b, (((1,), (1,)), ((), ())), preferred_element_type=F32)


def kernel(
    n, folded, groups_of_rows,
    ts_hbm, gains_hbm, bounds_hbm, band_hbm, taps_hbm, wafer_hbm, modes_hbm,
    out_ref, power_ref,
    ts_ref, gains_ref, bounds_ref, band_ref, taps_ref, wafer_ref, modes_ref, in_sem,
    own_ref, xh_ref, xm_ref, y_ref,
    a_ref, b_ref, p_ref, t_ref, sib_ref, got_ref, ssq_ref,
    sib_send, sib_recv, ring_send, ring_recv,
    psend, precv, tsend, trecv, qsend, qrecv,
):
    rows, samples = ts_hbm.shape
    half = samples // 2
    chips = n // 2
    hops = chips // 2
    blocks = samples // LANES
    part = rows // groups_of_rows
    bands, taps = taps_ref.shape
    wafers = modes_ref.shape[0]

    me = lax.axis_index("det")
    core = lax.rem(me, 2)
    chip = me // 2
    if folded:
        odd = lax.rem(chip, 2)
        ring = (1 - odd) * (chip // 2) + odd * (chips - 1 - chip // 2)
    else:
        ring = chip

    def chip_at(pos):
        pos = lax.rem(pos + 2 * chips, chips)
        if not folded:
            return pos
        late = pos // (chips // 2)
        return (1 - late) * 2 * pos + late * (2 * (chips - 1 - pos) + 1)

    step = 1 - 2 * core

    barrier = pltpu.get_barrier_semaphore()

    for near in (
        2 * chip + 1 - core,
        2 * chip_at(ring + 1) + core,
        2 * chip_at(ring - 1) + core,
    ):
        pl.semaphore_signal(barrier, inc=1, device_id={"det": near}, device_id_type=MESH)

    small = [
        pltpu.make_async_copy(src, dst, in_sem.at[i])
        for i, (src, dst) in enumerate(
            (
                (taps_hbm, taps_ref),
                (modes_hbm, modes_ref),
                (band_hbm, band_ref),
                (wafer_hbm, wafer_ref),
                (gains_hbm, gains_ref),
                (bounds_hbm, bounds_ref),
            )
        )
    ]
    large = [
        pltpu.make_async_copy(
            ts_hbm.at[pl.ds(g * part, part)],
            ts_ref.at[pl.ds(g * part, part)],
            in_sem.at[len(small) + g],
        )
        for g in range(groups_of_rows)
    ]
    for copy in small + large:
        copy.start()
    small[0].wait()

    depth = LANES + taps
    lag = (
        lax.broadcasted_iota(jnp.int32, (depth, LANES), 1)
        + taps
        - lax.broadcasted_iota(jnp.int32, (depth, LANES), 0)
    )
    mats = []
    for band in range(bands):
        mat = jnp.zeros((depth, LANES), F32)
        for k in range(taps):
            mat = jnp.where(lag == k, taps_ref[band, k], mat)
        mats.append(jnp.concatenate([jnp.zeros((LANES - taps, LANES), F32), mat], axis=0))
    toep_h, toep_m = split2(jnp.concatenate(mats, axis=1))

    for copy in small[1:]:
        copy.wait()

    eye = lax.broadcasted_iota(jnp.int32, (rows, rows), 0) == lax.broadcasted_iota(
        jnp.int32, (rows, rows), 1
    )

    def column(ref, i=0):
        row = ref[i : i + 1, :].astype(F32)
        return jnp.sum(jnp.where(eye, row, 0.0), axis=1, keepdims=True)

    band_col = column(band_ref)
    wafer_col = column(wafer_ref)
    gain_cols = [column(gains_ref, i) for i in range(gains_ref.shape[0])]
    bound_cols = [column(bounds_ref, i).astype(jnp.int32) for i in range(bounds_ref.shape[0])]

    modes = modes_ref[...]
    m1 = modes.astype(BF16).astype(F32)
    m2 = (modes - m1).astype(BF16).astype(F32)
    m3 = modes - m1 - m2
    stack = jnp.concatenate([m1, m2, m3], axis=0).astype(BF16)
    which = lax.rem(lax.broadcasted_iota(jnp.int32, (rows, 3 * wafers), 1), wafers)
    onehot = jnp.where(which.astype(F32) == wafer_col, 1.0, 0.0).astype(BF16)
    own_ref[...] = mm(onehot, stack)

    def ring_copy(d, g, who):
        span = pl.ds(g * part, part)
        src = a_ref.at[who, span] if d == 0 else b_ref.at[d - 1, who, span]
        return pltpu.make_async_remote_copy(
            src_ref=src,
            dst_ref=b_ref.at[d, who, span],
            send_sem=ring_send.at[d, who, g],
            recv_sem=ring_recv.at[d, who, g],
            device_id={"det": 2 * chip_at(ring + step) + core},
            device_id_type=MESH,
        )

    def sib_copy(g):
        span = pl.ds(g * part, part)
        return pltpu.make_async_remote_copy(
            src_ref=a_ref.at[2, span],
            dst_ref=a_ref.at[core, span],
            send_sem=sib_send.at[g],
            recv_sem=sib_recv.at[g],
            device_id={"det": 2 * chip + 1 - core},
            device_id_type=MESH,
        )

    def sib_arrival(g):
        span = pl.ds(g * part, part)
        return pltpu.make_async_remote_copy(
            src_ref=a_ref.at[2, span],
            dst_ref=a_ref.at[1 - core, span],
            send_sem=sib_send.at[g],
            recv_sem=sib_recv.at[g],
            device_id={"det": 2 * chip + 1 - core},
            device_id_type=MESH,
        )

    power = jnp.zeros((8, LANES), F32)
    sends = []
    for g in range(groups_of_rows):
        lo, hi = g * part, (g + 1) * part
        bound = [col[lo:hi] for col in bound_cols]
        gain = [col[lo:hi] for col in gain_cols]
        in_band = [band_col[lo:hi] == float(band) for band in range(bands)]
        large[g].wait()
        xh_ref[0:part, 0:LANES] = jnp.zeros((part, LANES), BF16)
        xm_ref[0:part, 0:LANES] = jnp.zeros((part, LANES), BF16)
        for blk in range(blocks):
            when = lax.broadcasted_iota(jnp.int32, (part, LANES), 1) + blk * LANES
            prof = jnp.broadcast_to(gain[0], (part, LANES))
            for c, edge in enumerate(bound):
                prof = jnp.where(when >= edge, gain[c + 1], prof)
            xh, xm = split2(ts_ref[lo:hi, blk * LANES : (blk + 1) * LANES] * prof)
            at = blk * part
            xh_ref[at : at + part, LANES:] = xh
            xm_ref[at : at + part, LANES:] = xm
            if blk + 1 < blocks:
                xh_ref[at + part : at + 2 * part, 0:LANES] = xh
                xm_ref[at + part : at + 2 * part, 0:LANES] = xm
        y_ref[...] = mm(xh_ref[...], toep_h) + (
            mm(xh_ref[...], toep_m) + mm(xm_ref[...], toep_h)
        )
        cross = jnp.zeros((part, LANES), F32)
        norm = jnp.zeros((part, LANES), F32)
        for blk in range(blocks):
            at = blk * part
            filt = y_ref[at : at + part, 0:LANES]
            for band in range(1, bands):
                filt = jnp.where(
                    in_band[band], y_ref[at : at + part, band * LANES : (band + 1) * LANES], filt
                )
            y_ref[at : at + part, 0:LANES] = filt
            mode = own_ref[lo:hi, blk * LANES : (blk + 1) * LANES]
            cross = cross + filt * mode
            norm = norm + mode * mode
        coupling = (jnp.sum(cross, axis=1, keepdims=True) / samples) / (
            jnp.sum(norm, axis=1, keepdims=True) / samples + 1e-06
        )
        sq = jnp.zeros((part, LANES), F32)
        for blk in range(blocks):
            at = blk * part
            second = blk >= blocks // 2
            slot = (2 - core) if second else 2 * core
            mode = own_ref[lo:hi, blk * LANES : (blk + 1) * LANES]
            clean = (y_ref[at : at + part, 0:LANES] - coupling * mode).astype(BF16)
            col = blk * LANES - (half if second else 0)
            a_ref[slot, lo:hi, col : col + LANES] = clean
            wide = clean.astype(F32)
            sq = sq + wide * wide
        for i in range(part // 8):
            power = power + sq[8 * i : 8 * i + 8]
        if g == 0:
            pl.semaphore_wait(barrier, 3)
        sib = sib_copy(g)
        sib.start()
        first = ring_copy(0, g, core)
        first.start()
        sends += [sib, first]

    for g in range(groups_of_rows):
        sib_arrival(g).wait_recv()
        second = ring_copy(0, g, 1 - core)
        second.start()
        sends.append(second)

    def swap_power(src, dst, i):
        return pltpu.make_async_remote_copy(
            src_ref=ssq_ref.at[src],
            dst_ref=ssq_ref.at[dst],
            send_sem=qsend.at[i],
            recv_sem=qrecv.at[i],
            device_id={"det": 2 * chip + 1 - core},
            device_id_type=MESH,
        )

    def pass_power(d):
        return pltpu.make_async_remote_copy(
            src_ref=ssq_ref.at[d],
            dst_ref=ssq_ref.at[d + 1],
            send_sem=qsend.at[2 + d],
            recv_sem=qrecv.at[2 + d],
            device_id={"det": 2 * chip_at(ring + step) + core},
            device_id_type=MESH,
        )

    ssq_ref[hops + 1] = power
    swap_first = swap_power(hops + 1, hops + 2, 0)
    swap_first.start()
    sends.append(swap_first)

    def give_sibling(d):
        return pltpu.make_async_remote_copy(
            src_ref=p_ref.at[d, 1 - core],
            dst_ref=sib_ref.at[d],
            send_sem=psend.at[d],
            recv_sem=precv.at[d],
            device_id={"det": 2 * chip + 1 - core},
            device_id_type=MESH,
        )

    def give_turned(d, to):
        return pltpu.make_async_remote_copy(
            src_ref=t_ref.at[d - 1, to],
            dst_ref=got_ref.at[core, d - 1],
            send_sem=tsend.at[d - 1, to],
            recv_sem=trecv.at[core, d - 1],
            device_id={"det": 2 * chip_at(ring - step * d) + to},
            device_id_type=MESH,
        )

    def take_turned(who, d):
        return pltpu.make_async_remote_copy(
            src_ref=t_ref.at[d - 1, 0],
            dst_ref=got_ref.at[who, d - 1],
            send_sem=tsend.at[d - 1, 0],
            recv_sem=trecv.at[who, d - 1],
            device_id={"det": 2 * chip + 1 - core},
            device_id_type=MESH,
        )

    mine = a_ref[0:2].reshape(2 * rows, half)

    def product(d):
        block = mine if d == 0 else b_ref[d - 1].reshape(2 * rows, half)
        prod = mm_t(mine, block)
        p_ref[d, 0] = prod[0:rows]
        p_ref[d, 1] = prod[rows:]
        give = give_sibling(d)
        give.start()
        sends.append(give)
        if 0 < d < hops:
            turned = prod.T
            t_ref[d - 1, 0] = turned[0:rows]
            t_ref[d - 1, 1] = turned[rows:]
            for to in range(2):
                give = give_turned(d, to)
                give.start()
                sends.append(give)

    product(0)
    swap_first.wait_recv()
    ssq_ref[0] = power + ssq_ref[hops + 2]
    onward = pass_power(0)
    onward.start()
    sends.append(onward)
    beside = jnp.zeros((8, LANES), F32)
    for d in range(1, hops + 1):
        for flip in range(2):
            who = core if flip == 0 else 1 - core
            for g in range(groups_of_rows):
                ring_copy(d - 1, g, who).wait_recv()
                if d < hops:
                    onward = ring_copy(d, g, who)
                    onward.start()
                    sends.append(onward)
        pass_power(d - 1).wait_recv()
        if d < hops:
            onward = pass_power(d)
            onward.start()
            sends.append(onward)
            beside = beside + ssq_ref[d]
        if d == hops - 1:
            ssq_ref[hops + 3] = beside
            swap_last = swap_power(hops + 3, hops + 4, 1)
            swap_last.start()
            sends.append(swap_last)
        product(d)

    swap_last.wait_recv()
    total = jnp.sum(ssq_ref[0] + beside + ssq_ref[hops + 4] + ssq_ref[hops])
    mean_power = total / float(rows * n * samples)
    power_ref[...] = jnp.full((8, LANES), mean_power, F32)

    def put(pos, value):
        col = pl.multiple_of(chip_at(pos) * (2 * rows), 2 * rows)
        out_ref[:, pl.ds(col, 2 * rows)] = value

    for d in range(hops + 1):
        give_sibling(d).wait_recv()
        if d == 0 or d == hops:
            put(ring + d, p_ref[d, core] + sib_ref[d])
        else:
            take_turned(1 - core, d).wait_recv()
            put(ring - step * d, p_ref[d, core] + got_ref[1 - core, d - 1])
            take_turned(core, d).wait_recv()
            put(ring + step * d, sib_ref[d] + got_ref[core, d - 1])

    for copy in sends:
        copy.wait_send()


def on_device(
    n, folded, timestream, seg_gains, seg_bounds, det_band, band_taps, det_wafer, wafer_modes
):
    rows, samples = timestream.shape
    half = samples // 2
    hops = n // 4
    pieces = 2
    part = rows // pieces
    bands = band_taps.shape[0]
    hbm = pl.BlockSpec(memory_space=pltpu.HBM)
    dma = pltpu.SemaphoreType.DMA
    gram, mean_power = pl.pallas_call(
        functools.partial(kernel, n, folded, pieces),
        out_shape=(
            jax.ShapeDtypeStruct((rows, rows * n), F32),
            jax.ShapeDtypeStruct((8, LANES), F32),
        ),
        in_specs=[hbm] * 7,
        out_specs=(pl.BlockSpec(memory_space=pltpu.VMEM),) * 2,
        scratch_shapes=[
            pltpu.VMEM((rows, samples), F32),
            pltpu.VMEM(seg_gains.shape[::-1], F32),
            pltpu.VMEM(seg_bounds.shape[::-1], jnp.int32),
            pltpu.VMEM((1, rows), jnp.int32),
            pltpu.SMEM(band_taps.shape, F32),
            pltpu.VMEM((1, rows), jnp.int32),
            pltpu.VMEM(wafer_modes.shape, F32),
            dma((6 + pieces,)),
            pltpu.VMEM((rows, samples), F32),
            pltpu.VMEM((part * samples // LANES, 2 * LANES), BF16),
            pltpu.VMEM((part * samples // LANES, 2 * LANES), BF16),
            pltpu.VMEM((part * samples // LANES, bands * LANES), F32),
            pltpu.VMEM((3, rows, half), BF16),
            pltpu.VMEM((hops, 2, rows, half), BF16),
            pltpu.VMEM((hops + 1, 2, rows, 2 * rows), F32),
            pltpu.VMEM((hops - 1, 2, rows, 2 * rows), F32),
            pltpu.VMEM((hops + 1, rows, 2 * rows), F32),
            pltpu.VMEM((2, hops - 1, rows, 2 * rows), F32),
            pltpu.VMEM((hops + 5, 8, LANES), F32),
            dma((pieces,)),
            dma((pieces,)),
            dma((hops, 2, pieces)),
            dma((hops, 2, pieces)),
            dma((hops + 1,)),
            dma((hops + 1,)),
            dma((hops - 1, 2)),
            dma((2, hops - 1)),
            dma((hops + 2,)),
            dma((hops + 2,)),
        ],
        compiler_params=pltpu.CompilerParams(
            collective_id=0, has_side_effects=True, vmem_limit_bytes=63 * 1024 * 1024
        ),
    )(
        timestream,
        seg_gains.T,
        seg_bounds.T,
        det_band.reshape(1, rows),
        band_taps,
        det_wafer.reshape(1, rows),
        wafer_modes,
    )
    return gram / (samples * mean_power[0, 0])


def solution(mesh):
    n = mesh.shape["det"]
    folded = mesh.shape["groups"] == 2
    return jax.shard_map(
        functools.partial(on_device, n, folded),
        mesh=mesh,
        in_specs=(
            P(("groups", "det"), None),
            P(("groups", "det"), None),
            P(("groups", "det"), None),
            P(("groups", "det")),
            P(),
            P(("groups", "det")),
            P("groups", None),
        ),
        out_specs=P(("groups", "det"), None),
        check_vma=False,
    )
```

```python
import functools

import jax
import jax.numpy as jnp
from jax import lax
from jax.experimental import pallas as pl
from jax.experimental.pallas import tpu as pltpu
from jax.sharding import PartitionSpec as P

F32 = jnp.float32
BF16 = jnp.bfloat16
LANES = 128
MESH = pl.DeviceIdType.MESH


def split2(x):
    high = x.astype(BF16)
    return high, (x - high.astype(F32)).astype(BF16)


def mm(a, b):
    return jnp.dot(a, b, preferred_element_type=F32)


def mm_t(a, b):
    return lax.dot_general(a, b, (((1,), (1,)), ((), ())), preferred_element_type=F32)


def kernel(
    n, folded, groups_of_rows,
    ts_hbm, gains_hbm, bounds_hbm, band_hbm, taps_hbm, wafer_hbm, modes_hbm,
    out_ref,
    ts_ref, gains_ref, bounds_ref, band_ref, taps_ref, wafer_ref, modes_ref, in_sem,
    own_ref, xh_ref, xm_ref, y_ref,
    a_ref, b_ref, p_ref, t_ref, sib_ref, got_ref, ssq_ref,
    sib_send, sib_recv, ring_send, ring_recv,
    psend, precv, tsend, trecv, qsend, qrecv,
):
    rows, samples = ts_hbm.shape
    half = samples // 2
    chips = n // 2
    hops = chips // 2
    blocks = samples // LANES
    part = rows // groups_of_rows
    bands, taps = taps_ref.shape
    wafers = modes_ref.shape[0]

    me = lax.axis_index("det")
    core = lax.rem(me, 2)
    chip = me // 2
    if folded:
        odd = lax.rem(chip, 2)
        ring = (1 - odd) * (chip // 2) + odd * (chips - 1 - chip // 2)
    else:
        ring = chip

    def chip_at(pos):
        pos = lax.rem(pos + 2 * chips, chips)
        if not folded:
            return pos
        late = pos // (chips // 2)
        return (1 - late) * 2 * pos + late * (2 * (chips - 1 - pos) + 1)

    step = 1 - 2 * core

    barrier = pltpu.get_barrier_semaphore()

    for near in (
        2 * chip + 1 - core,
        2 * chip_at(ring + 1) + core,
        2 * chip_at(ring - 1) + core,
    ):
        pl.semaphore_signal(barrier, inc=1, device_id={"det": near}, device_id_type=MESH)

    small = [
        pltpu.make_async_copy(src, dst, in_sem.at[i])
        for i, (src, dst) in enumerate(
            (
                (taps_hbm, taps_ref),
                (modes_hbm, modes_ref),
                (band_hbm, band_ref),
                (wafer_hbm, wafer_ref),
                (gains_hbm, gains_ref),
                (bounds_hbm, bounds_ref),
            )
        )
    ]
    large = [
        pltpu.make_async_copy(
            ts_hbm.at[pl.ds(g * part, part)],
            ts_ref.at[pl.ds(g * part, part)],
            in_sem.at[len(small) + g],
        )
        for g in range(groups_of_rows)
    ]
    for copy in small + large:
        copy.start()
    small[0].wait()

    depth = LANES + taps
    lag = (
        lax.broadcasted_iota(jnp.int32, (depth, LANES), 1)
        + taps
        - lax.broadcasted_iota(jnp.int32, (depth, LANES), 0)
    )
    mats = []
    for band in range(bands):
        mat = jnp.zeros((depth, LANES), F32)
        for k in range(taps):
            mat = jnp.where(lag == k, taps_ref[band, k], mat)
        mats.append(jnp.concatenate([jnp.zeros((LANES - taps, LANES), F32), mat], axis=0))
    toep_h, toep_m = split2(jnp.concatenate(mats, axis=1))

    for copy in small[1:]:
        copy.wait()

    eye = lax.broadcasted_iota(jnp.int32, (rows, rows), 0) == lax.broadcasted_iota(
        jnp.int32, (rows, rows), 1
    )

    def column(ref, i=0):
        row = ref[i : i + 1, :].astype(F32)
        return jnp.sum(jnp.where(eye, row, 0.0), axis=1, keepdims=True)

    band_col = column(band_ref)
    wafer_col = column(wafer_ref)
    gain_cols = [column(gains_ref, i) for i in range(gains_ref.shape[0])]
    bound_cols = [column(bounds_ref, i).astype(jnp.int32) for i in range(bounds_ref.shape[0])]

    modes = modes_ref[...]
    m1 = modes.astype(BF16).astype(F32)
    m2 = (modes - m1).astype(BF16).astype(F32)
    m3 = modes - m1 - m2
    stack = jnp.concatenate([m1, m2, m3], axis=0).astype(BF16)
    which = lax.rem(lax.broadcasted_iota(jnp.int32, (rows, 3 * wafers), 1), wafers)
    onehot = jnp.where(which.astype(F32) == wafer_col, 1.0, 0.0).astype(BF16)
    own_ref[...] = mm(onehot, stack)

    def ring_copy(d, g, who):
        span = pl.ds(g * part, part)
        src = a_ref.at[who, span] if d == 0 else b_ref.at[d - 1, who, span]
        return pltpu.make_async_remote_copy(
            src_ref=src,
            dst_ref=b_ref.at[d, who, span],
            send_sem=ring_send.at[d, who, g],
            recv_sem=ring_recv.at[d, who, g],
            device_id={"det": 2 * chip_at(ring + step) + core},
            device_id_type=MESH,
        )

    def sib_copy(g):
        span = pl.ds(g * part, part)
        return pltpu.make_async_remote_copy(
            src_ref=a_ref.at[2, span],
            dst_ref=a_ref.at[core, span],
            send_sem=sib_send.at[g],
            recv_sem=sib_recv.at[g],
            device_id={"det": 2 * chip + 1 - core},
            device_id_type=MESH,
        )

    def sib_arrival(g):
        span = pl.ds(g * part, part)
        return pltpu.make_async_remote_copy(
            src_ref=a_ref.at[2, span],
            dst_ref=a_ref.at[1 - core, span],
            send_sem=sib_send.at[g],
            recv_sem=sib_recv.at[g],
            device_id={"det": 2 * chip + 1 - core},
            device_id_type=MESH,
        )

    power = jnp.zeros((8, LANES), F32)
    sends = []
    for g in range(groups_of_rows):
        lo, hi = g * part, (g + 1) * part
        bound = [col[lo:hi] for col in bound_cols]
        gain = [col[lo:hi] for col in gain_cols]
        in_band = [band_col[lo:hi] == float(band) for band in range(bands)]
        large[g].wait()
        xh_ref[0:part, 0:LANES] = jnp.zeros((part, LANES), BF16)
        xm_ref[0:part, 0:LANES] = jnp.zeros((part, LANES), BF16)
        for blk in range(blocks):
            when = lax.broadcasted_iota(jnp.int32, (part, LANES), 1) + blk * LANES
            prof = jnp.broadcast_to(gain[0], (part, LANES))
            for c, edge in enumerate(bound):
                prof = jnp.where(when >= edge, gain[c + 1], prof)
            xh, xm = split2(ts_ref[lo:hi, blk * LANES : (blk + 1) * LANES] * prof)
            at = blk * part
            xh_ref[at : at + part, LANES:] = xh
            xm_ref[at : at + part, LANES:] = xm
            if blk + 1 < blocks:
                xh_ref[at + part : at + 2 * part, 0:LANES] = xh
                xm_ref[at + part : at + 2 * part, 0:LANES] = xm
        y_ref[...] = mm(xh_ref[...], toep_h) + (
            mm(xh_ref[...], toep_m) + mm(xm_ref[...], toep_h)
        )
        cross = jnp.zeros((part, LANES), F32)
        norm = jnp.zeros((part, LANES), F32)
        for blk in range(blocks):
            at = blk * part
            filt = y_ref[at : at + part, 0:LANES]
            for band in range(1, bands):
                filt = jnp.where(
                    in_band[band], y_ref[at : at + part, band * LANES : (band + 1) * LANES], filt
                )
            y_ref[at : at + part, 0:LANES] = filt
            mode = own_ref[lo:hi, blk * LANES : (blk + 1) * LANES]
            cross = cross + filt * mode
            norm = norm + mode * mode
        coupling = (jnp.sum(cross, axis=1, keepdims=True) / samples) / (
            jnp.sum(norm, axis=1, keepdims=True) / samples + 1e-06
        )
        sq = jnp.zeros((part, LANES), F32)
        for blk in range(blocks):
            at = blk * part
            second = blk >= blocks // 2
            slot = (2 - core) if second else 2 * core
            mode = own_ref[lo:hi, blk * LANES : (blk + 1) * LANES]
            clean = (y_ref[at : at + part, 0:LANES] - coupling * mode).astype(BF16)
            col = blk * LANES - (half if second else 0)
            a_ref[slot, lo:hi, col : col + LANES] = clean
            wide = clean.astype(F32)
            sq = sq + wide * wide
        for i in range(part // 8):
            power = power + sq[8 * i : 8 * i + 8]
        if g == 0:
            pl.semaphore_wait(barrier, 3)
        sib = sib_copy(g)
        sib.start()
        first = ring_copy(0, g, core)
        first.start()
        sends += [sib, first]

    for g in range(groups_of_rows):
        sib_arrival(g).wait_recv()
        second = ring_copy(0, g, 1 - core)
        second.start()
        sends.append(second)

    def swap_power(src, dst, i):
        return pltpu.make_async_remote_copy(
            src_ref=ssq_ref.at[src],
            dst_ref=ssq_ref.at[dst],
            send_sem=qsend.at[i],
            recv_sem=qrecv.at[i],
            device_id={"det": 2 * chip + 1 - core},
            device_id_type=MESH,
        )

    def pass_power(d):
        return pltpu.make_async_remote_copy(
            src_ref=ssq_ref.at[d],
            dst_ref=ssq_ref.at[d + 1],
            send_sem=qsend.at[2 + d],
            recv_sem=qrecv.at[2 + d],
            device_id={"det": 2 * chip_at(ring + step) + core},
            device_id_type=MESH,
        )

    ssq_ref[hops + 1] = power
    swap_first = swap_power(hops + 1, hops + 2, 0)
    swap_first.start()
    sends.append(swap_first)

    def give_sibling(d):
        return pltpu.make_async_remote_copy(
            src_ref=p_ref.at[d, 1 - core],
            dst_ref=sib_ref.at[d],
            send_sem=psend.at[d],
            recv_sem=precv.at[d],
            device_id={"det": 2 * chip + 1 - core},
            device_id_type=MESH,
        )

    def give_turned(d, to):
        return pltpu.make_async_remote_copy(
            src_ref=t_ref.at[d - 1, to],
            dst_ref=got_ref.at[core, d - 1],
            send_sem=tsend.at[d - 1, to],
            recv_sem=trecv.at[core, d - 1],
            device_id={"det": 2 * chip_at(ring - step * d) + to},
            device_id_type=MESH,
        )

    def take_turned(who, d):
        return pltpu.make_async_remote_copy(
            src_ref=t_ref.at[d - 1, 0],
            dst_ref=got_ref.at[who, d - 1],
            send_sem=tsend.at[d - 1, 0],
            recv_sem=trecv.at[who, d - 1],
            device_id={"det": 2 * chip + 1 - core},
            device_id_type=MESH,
        )

    mine = a_ref[0:2].reshape(2 * rows, half)

    def product(d):
        block = mine if d == 0 else b_ref[d - 1].reshape(2 * rows, half)
        prod = mm_t(mine, block)
        p_ref[d, 0] = prod[0:rows]
        p_ref[d, 1] = prod[rows:]
        give = give_sibling(d)
        give.start()
        sends.append(give)
        if 0 < d < hops:
            turned = prod.T
            t_ref[d - 1, 0] = turned[0:rows]
            t_ref[d - 1, 1] = turned[rows:]
            for to in range(2):
                give = give_turned(d, to)
                give.start()
                sends.append(give)

    product(0)
    swap_first.wait_recv()
    ssq_ref[0] = power + ssq_ref[hops + 2]
    onward = pass_power(0)
    onward.start()
    sends.append(onward)
    beside = jnp.zeros((8, LANES), F32)
    for d in range(1, hops + 1):
        for flip in range(2):
            who = core if flip == 0 else 1 - core
            for g in range(groups_of_rows):
                ring_copy(d - 1, g, who).wait_recv()
                if d < hops:
                    onward = ring_copy(d, g, who)
                    onward.start()
                    sends.append(onward)
        pass_power(d - 1).wait_recv()
        if d < hops:
            onward = pass_power(d)
            onward.start()
            sends.append(onward)
            beside = beside + ssq_ref[d]
        if d == hops - 1:
            ssq_ref[hops + 3] = beside
            swap_last = swap_power(hops + 3, hops + 4, 1)
            swap_last.start()
            sends.append(swap_last)
        product(d)

    swap_last.wait_recv()
    total = jnp.sum(ssq_ref[0] + beside + ssq_ref[hops + 4] + ssq_ref[hops])
    mean_power = total / float(rows * n * samples)
    scale = 1.0 / (samples * jnp.full((rows, LANES), mean_power, F32))

    def put(pos, value):
        col = pl.multiple_of(chip_at(pos) * (2 * rows), 2 * rows)
        out_ref[:, pl.ds(col, 2 * rows)] = value * scale

    for d in range(hops + 1):
        give_sibling(d).wait_recv()
        if d == 0 or d == hops:
            put(ring + d, p_ref[d, core] + sib_ref[d])
        else:
            take_turned(1 - core, d).wait_recv()
            put(ring - step * d, p_ref[d, core] + got_ref[1 - core, d - 1])
            take_turned(core, d).wait_recv()
            put(ring + step * d, sib_ref[d] + got_ref[core, d - 1])

    for copy in sends:
        copy.wait_send()


def on_device(
    n, folded, timestream, seg_gains, seg_bounds, det_band, band_taps, det_wafer, wafer_modes
):
    rows, samples = timestream.shape
    half = samples // 2
    hops = n // 4
    pieces = 2
    part = rows // pieces
    bands = band_taps.shape[0]
    hbm = pl.BlockSpec(memory_space=pltpu.HBM)
    dma = pltpu.SemaphoreType.DMA
    return pl.pallas_call(
        functools.partial(kernel, n, folded, pieces),
        out_shape=jax.ShapeDtypeStruct((rows, rows * n), F32),
        in_specs=[hbm] * 7,
        out_specs=pl.BlockSpec(memory_space=pltpu.VMEM),
        scratch_shapes=[
            pltpu.VMEM((rows, samples), F32),
            pltpu.VMEM(seg_gains.shape[::-1], F32),
            pltpu.VMEM(seg_bounds.shape[::-1], jnp.int32),
            pltpu.VMEM((1, rows), jnp.int32),
            pltpu.SMEM(band_taps.shape, F32),
            pltpu.VMEM((1, rows), jnp.int32),
            pltpu.VMEM(wafer_modes.shape, F32),
            dma((6 + pieces,)),
            pltpu.VMEM((rows, samples), F32),
            pltpu.VMEM((part * samples // LANES, 2 * LANES), BF16),
            pltpu.VMEM((part * samples // LANES, 2 * LANES), BF16),
            pltpu.VMEM((part * samples // LANES, bands * LANES), F32),
            pltpu.VMEM((3, rows, half), BF16),
            pltpu.VMEM((hops, 2, rows, half), BF16),
            pltpu.VMEM((hops + 1, 2, rows, 2 * rows), F32),
            pltpu.VMEM((hops - 1, 2, rows, 2 * rows), F32),
            pltpu.VMEM((hops + 1, rows, 2 * rows), F32),
            pltpu.VMEM((2, hops - 1, rows, 2 * rows), F32),
            pltpu.VMEM((hops + 5, 8, LANES), F32),
            dma((pieces,)),
            dma((pieces,)),
            dma((hops, 2, pieces)),
            dma((hops, 2, pieces)),
            dma((hops + 1,)),
            dma((hops + 1,)),
            dma((hops - 1, 2)),
            dma((2, hops - 1)),
            dma((hops + 2,)),
            dma((hops + 2,)),
        ],
        compiler_params=pltpu.CompilerParams(
            collective_id=0, has_side_effects=True, vmem_limit_bytes=63 * 1024 * 1024
        ),
    )(
        timestream,
        seg_gains.T,
        seg_bounds.T,
        det_band.reshape(1, rows),
        band_taps,
        det_wafer.reshape(1, rows),
        wafer_modes,
    )


def solution(mesh):
    n = mesh.shape["det"]
    folded = mesh.shape["groups"] == 2
    return jax.shard_map(
        functools.partial(on_device, n, folded),
        mesh=mesh,
        in_specs=(
            P(("groups", "det"), None),
            P(("groups", "det"), None),
            P(("groups", "det"), None),
            P(("groups", "det")),
            P(),
            P(("groups", "det")),
            P("groups", None),
        ),
        out_specs=P(("groups", "det"), None),
        check_vma=False,
    )
```
